32 devices in a mesh: ctx: 8 (over y, x, core), tp: 4 (over z).
Axes of the slice: x: 2, y: 2, z: 4, core: 2. Of those that a mesh axis runs over, the one named last changes fastest.
Arguments:
- attention: bfloat16 [4096, 2048], P('ctx', 'tp'), may hold values from -6 to 6
- residual: bfloat16 [4096, 2048], P(('ctx', 'tp')), may hold values from -6 to 6
- w_out: bfloat16 [2048, 2048], P('tp'), may hold values from -0.125 to 0.125
- w_qkv: bfloat16 [3072, 2048], P('tp'), may hold values from -0.125 to 0.125
- norm_moe: float32 [2048], replicated, may hold values from 0.25 to 1.75
- norm_attn: float32 [2048], replicated, may hold values from 0.25 to 1.75
- expert_ids: int32 [4096, 4], P(('ctx', 'tp')), may hold values from 0 to 15, all different within a row; in each aligned block of 128 rows (0 to 127, 128 to 255, ...) at most 48 rows name the same one
- expert_gates: float32 [4096, 4], P(('ctx', 'tp')), may hold values from 0.02 to 0.3
- w_gate: bfloat16 [32, 2048, 384], P(('ctx', 'tp')), may hold values from -0.125 to 0.125
- w_up: bfloat16 [32, 2048, 384], P(('ctx', 'tp')), may hold values from -0.125 to 0.125
- w_down: bfloat16 [32, 384, 2048], P(('ctx', 'tp')), may hold values from -0.21875 to 0.21875
- d_projected: bfloat16 [4096, 3072], P('ctx', 'tp'), may hold values from -6 to 6
- d_stream: bfloat16 [4096, 2048], P(('ctx', 'tp')), may hold values from -6 to 6
Outputs:
- projected: bfloat16 [4096, 3072], P('ctx', 'tp')
- stream: bfloat16 [4096, 2048], P(('ctx', 'tp'))
- grad_attention: bfloat16 [4096, 2048], P('ctx', 'tp')
- grad_residual: bfloat16 [4096, 2048], P(('ctx', 'tp'))
- grad_w_out: bfloat16 [2048, 2048], P('tp', 'ctx')
- grad_w_gate: bfloat16 [32, 2048, 384], P(('ctx', 'tp'))
- grad_w_up: bfloat16 [32, 2048, 384], P(('ctx', 'tp'))
- grad_w_down: bfloat16 [32, 384, 2048], P(('ctx', 'tp'))
The draws below stay inside these ranges and needn't reach their ends.
Inputs may be any that keep to these rules, and one draw needn't show every extreme that they name: `expert_ids`: each row names 4 different experts. Among the rows of one device no expert is named more than 48 times, a bound that some block reaches there.
All inputs are finite; a program needn't handle non-finite values.
Results may differ from the reference program's by a relative error of at most 0.0075.
Values may be sent and summed in bfloat16 or wider, within the bound.
A program may use at most 128 MiB of HBM per device.

```python
import math
import jax
import jax.numpy as jnp
import numpy as np
from jax import lax

D = 2048
FF = 768
TOPK = 4
QD = 2048
QKV = 3072
TOK_DEV = 512
TOKENS = 4096
EXPERTS = 16
HALVES = 32
CAP = 48
N_CTX = 8
N_TP = 4


def block_scale(key, shape, cuts, smallest, top_value):
    def one(dim, blocks):
        draws = jax.random.uniform(jax.random.fold_in(jax.random.fold_in(key, 6), dim), (blocks,), jnp.float32, smallest / len(cuts), top_value / len(cuts))
        return jnp.repeat(jnp.exp(draws), shape[dim] // blocks).reshape((-1,) + (1,) * (len(shape) - dim - 1))

    gain = one(*cuts[0])
    for cut in cuts[1:]:
        gain = gain * one(*cut)
    return gain


def assign_block(key, own, number, rows, number_of, top, most, lean):
    sequence = jax.random.permutation(key, number_of)
    crowded, ordinary = shares(number_of, rows * top, most, lean, True), shares(number_of, rows * top, most, lean, False)
    places = jnp.arange(number_of)

    def named(sizes, turn):
        used = int((sizes > 0).sum())
        fixed = max(1, used // 4)
        shifted = fixed + (places - fixed + turn * (used - fixed)) % max(1, number_of - fixed)
        return jnp.zeros((number_of,), jnp.int32).at[sequence[jnp.where(places < fixed, places, shifted)]].set(jnp.asarray(sizes, jnp.int32))

    sizes = jnp.where(number % 4 == 0, named(crowded, number // 4), named(ordinary, number - number // 4 - 1))
    mixed = jax.random.permutation(jax.random.fold_in(own, 3), number_of)
    donor, sink = mixed[0:number_of // 2 * 2:2], mixed[1:number_of // 2 * 2:2]
    margin = jnp.minimum(sizes[donor] - 1, most - sizes[sink]) // 2
    margin = jnp.where((donor == sequence[0]) | (sink == sequence[0]) | (sizes[sink] == 0), 0, jnp.maximum(margin, 0))
    shifted = jax.random.randint(jax.random.fold_in(own, 4), (number_of // 2,), 0, 1 << 20) % (margin + 1)
    sizes = sizes.at[donor].add(-shifted).at[sink].add(shifted)
    members = jnp.searchsorted(jnp.cumsum(sizes), jnp.arange(rows * top), side="right").astype(jnp.int32)
    listing = members.reshape(top, rows).T
    listing = listing[jax.random.permutation(jax.random.fold_in(own, 1), rows)]
    turn = jax.random.randint(jax.random.fold_in(own, 2), (rows, 1), 0, top)
    return jnp.take_along_axis(listing, (jnp.arange(top)[None, :] + turn) % top, axis=1)


def shares(amount, total, reach, slope, full):
    portions = [(1 << 20) // math.isqrt(grade ** slope) + 1 for grade in range(1, amount + 1)]
    largest = reach if full else min(reach, max(-(-total // amount), total * portions[0] // sum(portions)))
    least = 1 if total - largest >= amount - 1 else 0
    counts, spare = [largest] + [least] * (amount - 1), total - largest - least * (amount - 1)
    while spare > 0:
        free = [i for i in range(1, amount) if counts[i] < largest] or [i for i in range(1, amount) if counts[i] < reach]
        whole, budget = sum([portions[i] for i in free]), spare
        for i in free:
            more = min(reach - counts[i], max(1, budget * portions[i] // whole), spare)
            counts[i] = counts[i] + more
            spare = spare - more
    return np.array(counts)


def centred(key, shape, width, bound, split=(), kind=jnp.bfloat16):
    factor_of = block_scale(key, shape, split, -0.22, 0.18) if split else 1.0
    entries = jax.random.normal(key, shape, jnp.float32) * width * factor_of
    return jnp.minimum(jnp.maximum(entries, -bound), bound).astype(kind)


def setup_inputs(seed: int = 0) -> dict:
    splits = jax.random.split(jax.random.key(seed), 14)
    attention = centred(splits[0], (TOKENS, QD), 1.0, 6.0, ((0, 8), (1, 4)))
    residual = centred(splits[1], (TOKENS, D), 1.0, 6.0, ((0, 32),))
    w_out = centred(splits[2], (QD, D), QD ** -0.5, 0.125, ((0, 4),))
    w_qkv = centred(splits[3], (QKV, D), D ** -0.5, 0.125, ((0, 4),))
    norm_moe = jnp.clip(1.0 + 0.15 * jax.random.normal(splits[4], (D,), jnp.float32), 0.25, 1.75)
    norm_attn = jnp.clip(1.0 + 0.15 * jax.random.normal(splits[5], (D,), jnp.float32), 0.25, 1.75)
    expert_ids_keys = jax.random.split(jax.random.fold_in(splits[6], 1), TOKENS // (TOK_DEV // N_TP))
    expert_ids_turns = jax.random.permutation(jax.random.fold_in(splits[6], 3), TOKENS // (TOK_DEV // N_TP))
    expert_ids = jax.vmap(lambda own, number: assign_block(jax.random.fold_in(splits[6], 2), own, number, TOK_DEV // N_TP, EXPERTS, TOPK, CAP, 2))(expert_ids_keys, expert_ids_turns).reshape((TOKENS, TOPK))
    expert_gates = jnp.clip(0.02 + 0.28 * jax.random.uniform(splits[7], (TOKENS, TOPK), jnp.float32) ** block_scale(splits[7], (TOKENS, TOPK), ((0, 32),), -0.2, 0.2), 0.02, 0.3)
    w_gate = centred(splits[8], (HALVES, D, FF // 2), D ** -0.5, 0.125, ((0, 32),))
    w_up = centred(splits[9], (HALVES, D, FF // 2), D ** -0.5, 0.125, ((0, 32),))
    w_down = centred(splits[10], (HALVES, FF // 2, D), FF ** -0.5, 0.21875, ((0, 32),))
    d_projected = centred(splits[11], (TOKENS, QKV), 1.0, 6.0, ((0, 8), (1, 4)))
    d_stream = centred(splits[12], (TOKENS, D), 1.0, 6.0, ((0, 32),))
    return {"attention": attention, "residual": residual, "w_out": w_out, "w_qkv": w_qkv, "norm_moe": norm_moe, "norm_attn": norm_attn, "expert_ids": expert_ids, "expert_gates": expert_gates, "w_gate": w_gate, "w_up": w_up, "w_down": w_down, "d_projected": d_projected, "d_stream": d_stream}


EPSILON = 1e-06

def rms_inverse(hidden):
    return lax.rsqrt(lax.optimization_barrier(jnp.mean(hidden * hidden, axis=-1, keepdims=True)) + EPSILON)

def rms_grad(hidden, gain_vec, inv_rms, grad_out):
    normed = hidden * inv_rms
    grad_normed = grad_out * gain_vec
    return inv_rms * (grad_normed - normed * lax.optimization_barrier(jnp.mean(grad_normed * normed, axis=-1, keepdims=True)))

def expert_inner(slot_rows, gate_mat, up_mat):
    pre_gate = jnp.dot(slot_rows, gate_mat, preferred_element_type=jnp.float32)
    pre_up = jnp.dot(slot_rows, up_mat, preferred_element_type=jnp.float32)
    active = (jax.nn.silu(pre_gate) * pre_up).astype(jnp.bfloat16)
    return (pre_gate, pre_up, active)

def half_backward(slot_rows, slot_grads, pre_gate, pre_up, active, gate_mat, up_mat, down_mat):
    sigmoid_gate = jax.nn.sigmoid(pre_gate)
    silu_gate = pre_gate * sigmoid_gate
    grad_active = jnp.einsum('sd,fd->sf', slot_grads, down_mat, preferred_element_type=jnp.float32)
    grad_gate = (grad_active * pre_up * sigmoid_gate * (1.0 + pre_gate * (1.0 - sigmoid_gate))).astype(jnp.bfloat16)
    grad_up = (grad_active * silu_gate).astype(jnp.bfloat16)
    input_part = jnp.einsum('sf,df->sd', grad_gate, gate_mat, preferred_element_type=jnp.float32)
    input_part = (input_part + jnp.einsum('sf,df->sd', grad_up, up_mat, preferred_element_type=jnp.float32)).astype(jnp.bfloat16)
    gate_term = jnp.einsum('sd,sf->df', slot_rows, grad_gate, preferred_element_type=jnp.float32)
    up_term = jnp.einsum('sd,sf->df', slot_rows, grad_up, preferred_element_type=jnp.float32)
    down_term = jnp.einsum('sf,sd->fd', active, slot_grads, preferred_element_type=jnp.float32)
    return (input_part, gate_term, up_term, down_term)

def slot_tables(expert_ids, expert_gates):
    devices = N_CTX * N_TP
    per_device = TOKENS // devices
    blocks = expert_ids.reshape(devices, per_device * TOPK)
    expert_range = jnp.arange(EXPERTS, dtype=jnp.int32)
    onehot = (blocks[:, :, None] == expert_range[None, None, :]).astype(jnp.int32)
    position = lax.optimization_barrier(jnp.sum((jnp.cumsum(onehot, axis=1) - onehot) * onehot, axis=2))
    device_of = jnp.arange(devices, dtype=jnp.int32)[:, None]
    column = (device_of * CAP + position).reshape(-1).astype(jnp.int32)
    token_index = (jnp.arange(TOKENS * TOPK, dtype=jnp.int32) // TOPK).astype(jnp.int32)
    flat_ids = expert_ids.reshape(-1)
    token_of = jnp.full((EXPERTS, devices * CAP), TOKENS, jnp.int32).at[flat_ids, column].set(token_index)
    gate_of = jnp.zeros((EXPERTS, devices * CAP), jnp.float32).at[flat_ids, column].set(expert_gates.reshape(-1))
    return (token_of, gate_of)

def reference(attention, residual, w_out, w_qkv, norm_moe, norm_attn, expert_ids, expert_gates, w_gate, w_up, w_down, d_projected, d_stream):
    half_width = FF // 2
    hidden = residual.astype(jnp.float32) + jnp.dot(attention, w_out, preferred_element_type=jnp.float32)
    inv_one = rms_inverse(hidden)
    moe_input = (hidden * inv_one * norm_moe).astype(jnp.bfloat16)
    token_of, gate_of = slot_tables(expert_ids, expert_gates)
    input_pad = jnp.concatenate([moe_input, jnp.zeros((1, D), jnp.bfloat16)], axis=0)
    gate_pairs = w_gate.reshape(EXPERTS, 2, D, half_width)
    up_pairs = w_up.reshape(EXPERTS, 2, D, half_width)
    down_pairs = w_down.reshape(EXPERTS, 2, half_width, D)

    def forward_expert(running, inputs):
        gate_pair, up_pair, down_pair, tokens_here, gates_here = inputs
        slot_rows = input_pad[tokens_here]
        first = jnp.dot(expert_inner(slot_rows, gate_pair[0], up_pair[0])[2], down_pair[0], preferred_element_type=jnp.float32).astype(jnp.bfloat16)
        second = jnp.dot(expert_inner(slot_rows, gate_pair[1], up_pair[1])[2], down_pair[1], preferred_element_type=jnp.float32).astype(jnp.bfloat16)
        output = (first.astype(jnp.float32) + second.astype(jnp.float32)).astype(jnp.bfloat16)
        return (running.at[tokens_here].add(gates_here[:, None] * output.astype(jnp.float32)), None)
    moe_sum = lax.scan(forward_expert, jnp.zeros((TOKENS + 1, D), jnp.float32), (gate_pairs, up_pairs, down_pairs, token_of, gate_of))[0]
    stream_sum = hidden + moe_sum[:TOKENS]
    stream = stream_sum.astype(jnp.bfloat16)
    inv_two = rms_inverse(stream_sum)
    attn_input = (stream_sum * inv_two * norm_attn).astype(jnp.bfloat16)
    projected = jnp.dot(attn_input, w_qkv.T, preferred_element_type=jnp.float32).astype(jnp.bfloat16)
    grad_attn_in = jnp.dot(d_projected, w_qkv, preferred_element_type=jnp.float32)
    grad_stream = d_stream.astype(jnp.float32) + rms_grad(stream_sum, norm_attn, inv_two, grad_attn_in)
    grad_pad = jnp.concatenate([grad_stream, jnp.zeros((1, D), jnp.float32)], axis=0)

    def backward_expert(running, inputs):
        gate_pair, up_pair, down_pair, tokens_here, gates_here = inputs
        slot_rows = input_pad[tokens_here]
        slot_grads = (gates_here[:, None] * grad_pad[tokens_here]).astype(jnp.bfloat16)
        parts = []
        gate_terms = []
        up_terms = []
        down_terms = []
        for half in range(2):
            pre_gate, pre_up, active = expert_inner(slot_rows, gate_pair[half], up_pair[half])
            input_part, gate_term, up_term, down_term = half_backward(slot_rows, slot_grads, pre_gate, pre_up, active, gate_pair[half], up_pair[half], down_pair[half])
            parts.append(input_part.astype(jnp.float32))
            gate_terms.append(gate_term.astype(jnp.bfloat16))
            up_terms.append(up_term.astype(jnp.bfloat16))
            down_terms.append(down_term.astype(jnp.bfloat16))
        grad_input = (parts[0] + parts[1]).astype(jnp.bfloat16)
        stacked = (jnp.stack(gate_terms), jnp.stack(up_terms), jnp.stack(down_terms))
        return (running.at[tokens_here].add(grad_input.astype(jnp.float32)), stacked)
    grad_moe_pad, weight_grads = lax.scan(backward_expert, jnp.zeros((TOKENS + 1, D), jnp.float32), (gate_pairs, up_pairs, down_pairs, token_of, gate_of))
    grad_hidden = grad_stream + rms_grad(hidden, norm_moe, inv_one, grad_moe_pad[:TOKENS])
    grad_residual = grad_hidden.astype(jnp.bfloat16)
    grad_attention = jnp.dot(grad_residual, w_out.T, preferred_element_type=jnp.float32).astype(jnp.bfloat16)
    grad_w_out = jnp.dot(attention.T, grad_residual, preferred_element_type=jnp.float32).astype(jnp.bfloat16)
    grad_w_gate = weight_grads[0].reshape(HALVES, D, half_width)
    grad_w_up = weight_grads[1].reshape(HALVES, D, half_width)
    grad_w_down = weight_grads[2].reshape(HALVES, half_width, D)
    return (projected, stream, grad_attention, grad_residual, grad_w_out, grad_w_gate, grad_w_up, grad_w_down)
```

```python
import jax
import jax.numpy as jnp
from jax import lax
from jax.sharding import PartitionSpec as P

EPSILON = 1e-06


def rms_inverse(hidden):
    return lax.rsqrt(jnp.mean(hidden * hidden, axis=-1, keepdims=True) + EPSILON)


def rms_grad(hidden, gain_vec, inv_rms, grad_out):
    normed = hidden * inv_rms
    grad_normed = grad_out * gain_vec
    return inv_rms * (grad_normed - normed * jnp.mean(grad_normed * normed, axis=-1, keepdims=True))


def expert_inner(slot_rows, gate_mat, up_mat):
    pre_gate = jnp.dot(slot_rows, gate_mat, preferred_element_type=jnp.float32)
    pre_up = jnp.dot(slot_rows, up_mat, preferred_element_type=jnp.float32)
    active = (jax.nn.silu(pre_gate) * pre_up).astype(jnp.bfloat16)
    return (pre_gate, pre_up, active)


def half_backward(slot_rows, slot_grads, pre_gate, pre_up, active, gate_mat, up_mat, down_mat):
    sigmoid_gate = jax.nn.sigmoid(pre_gate)
    silu_gate = pre_gate * sigmoid_gate
    grad_active = jnp.einsum("sd,fd->sf", slot_grads, down_mat, preferred_element_type=jnp.float32)
    grad_gate = (
        grad_active * pre_up * sigmoid_gate * (1.0 + pre_gate * (1.0 - sigmoid_gate))
    ).astype(jnp.bfloat16)
    grad_up = (grad_active * silu_gate).astype(jnp.bfloat16)
    input_part = jnp.einsum("sf,df->sd", grad_gate, gate_mat, preferred_element_type=jnp.float32)
    input_part = (
        input_part + jnp.einsum("sf,df->sd", grad_up, up_mat, preferred_element_type=jnp.float32)
    ).astype(jnp.bfloat16)
    gate_term = jnp.einsum("sd,sf->df", slot_rows, grad_gate, preferred_element_type=jnp.float32)
    up_term = jnp.einsum("sd,sf->df", slot_rows, grad_up, preferred_element_type=jnp.float32)
    down_term = jnp.einsum("sf,sd->fd", active, slot_grads, preferred_element_type=jnp.float32)
    return (input_part, gate_term, up_term, down_term)


def tensor_rows(local_sum):
    return lax.psum_scatter(
        local_sum.astype(jnp.bfloat16), "tp", scatter_dimension=0, tiled=True
    ).astype(jnp.float32)


def group_rows(local_rows):
    return lax.all_gather(local_rows, "tp", axis=0, tiled=True)


def exchange(blocks):
    return lax.all_to_all(blocks, "ctx", split_axis=0, concat_axis=0, tiled=True)


def local(
    attention,
    residual,
    w_out,
    w_qkv,
    norm_moe,
    norm_attn,
    expert_ids,
    expert_gates,
    w_gate,
    w_up,
    w_down,
    d_projected,
    d_stream,
):
    ctx_count = lax.axis_size("ctx")
    tensor_count = lax.axis_size("tp")
    group_tokens = attention.shape[0]
    local_tokens = group_tokens // tensor_count
    model_width = residual.shape[1]
    expert_count = ctx_count * tensor_count // 2
    top_count = expert_ids.shape[1]
    capacity = 2 * max(1, local_tokens * top_count * 3 // (4 * expert_count))
    group_cap = tensor_count * capacity
    slot_count = ctx_count * group_cap
    gate_mat = w_gate[0]
    up_mat = w_up[0]
    down_mat = w_down[0]

    routing = group_rows(
        jnp.concatenate([expert_ids.astype(jnp.float32), expert_gates], axis=1)
    )
    group_ids = routing[:, :top_count].astype(jnp.int32)
    group_gates = routing[:, top_count:]
    targets = (jnp.arange(ctx_count, dtype=jnp.int32) * tensor_count + lax.axis_index("tp")) // 2
    named = group_ids[:, None, :] == targets[None, :, None]
    member = jnp.any(named, axis=2)
    gate_of = jnp.sum(jnp.where(named, group_gates[:, None, :], 0.0), axis=2)
    token_range = jnp.arange(group_tokens, dtype=jnp.int32)
    earlier = (token_range[:, None] > token_range[None, :]).astype(jnp.bfloat16)
    position = jnp.dot(
        earlier, member.astype(jnp.bfloat16), preferred_element_type=jnp.float32
    ).astype(jnp.int32)
    slot_of = jnp.where(member, position, -1).T
    taken = slot_of[:, None, :] == jnp.arange(group_cap, dtype=jnp.int32)[None, :, None]
    select = taken.astype(jnp.bfloat16).reshape(slot_count, group_tokens)
    weighted = jnp.where(taken, gate_of.T[:, None, :], 0.0)
    slot_gate = jnp.sum(weighted, axis=2).reshape(slot_count, 1)
    weighted = weighted.astype(jnp.bfloat16).reshape(slot_count, group_tokens)

    def to_experts(rows):
        return exchange(rows.reshape(ctx_count, group_cap, model_width)).reshape(
            slot_count, model_width
        )

    grad_attn_in = tensor_rows(
        jnp.dot(d_projected, w_qkv, preferred_element_type=jnp.float32)
    )
    hidden = residual.astype(jnp.float32) + tensor_rows(
        jnp.dot(attention, w_out, preferred_element_type=jnp.float32)
    )
    inv_one = rms_inverse(hidden)
    moe_input = group_rows((hidden * inv_one * norm_moe).astype(jnp.bfloat16))
    arrived = to_experts(
        jnp.dot(select, moe_input, preferred_element_type=jnp.float32).astype(jnp.bfloat16)
    )
    pre_gate, pre_up, active = expert_inner(arrived, gate_mat, up_mat)
    half_out = jnp.dot(active, down_mat, preferred_element_type=jnp.float32).astype(jnp.bfloat16)
    returned = to_experts(half_out)
    moe_out = tensor_rows(
        jnp.einsum("st,sd->td", weighted, returned, preferred_element_type=jnp.float32)
    )
    stream_sum = hidden + moe_out
    stream = stream_sum.astype(jnp.bfloat16)
    inv_two = rms_inverse(stream_sum)
    grad_stream = d_stream.astype(jnp.float32) + rms_grad(
        stream_sum, norm_attn, inv_two, grad_attn_in
    )
    grad_rows = group_rows(grad_stream.astype(jnp.bfloat16))
    grad_slots = jnp.dot(select, grad_rows, preferred_element_type=jnp.float32) * slot_gate
    grad_arrived = to_experts(grad_slots.astype(jnp.bfloat16))
    attn_rows = group_rows((stream_sum * inv_two * norm_attn).astype(jnp.bfloat16))
    projected = jnp.einsum(
        "td,od->to", attn_rows, w_qkv, preferred_element_type=jnp.float32
    ).astype(jnp.bfloat16)
    input_part, gate_grad, up_grad, down_grad = half_backward(
        arrived, grad_arrived, pre_gate, pre_up, active, gate_mat, up_mat, down_mat
    )
    back_rows = to_experts(input_part)
    grad_moe_in = tensor_rows(
        jnp.einsum("st,sd->td", select, back_rows, preferred_element_type=jnp.float32)
    )
    grad_hidden = grad_stream + rms_grad(hidden, norm_moe, inv_one, grad_moe_in)
    grad_residual = grad_hidden.astype(jnp.bfloat16)
    grad_rows_all = group_rows(grad_residual)
    grad_attention = jnp.einsum(
        "td,kd->tk", grad_rows_all, w_out, preferred_element_type=jnp.float32
    ).astype(jnp.bfloat16)
    out_partial = jnp.einsum(
        "tk,td->kd", attention, grad_rows_all, preferred_element_type=jnp.float32
    )
    out_weight_grad = lax.psum_scatter(
        out_partial.astype(jnp.bfloat16), "ctx", scatter_dimension=1, tiled=True
    )
    return (
        projected,
        stream,
        grad_attention,
        grad_residual,
        out_weight_grad,
        gate_grad.astype(jnp.bfloat16)[None],
        up_grad.astype(jnp.bfloat16)[None],
        down_grad.astype(jnp.bfloat16)[None],
    )


def solution(mesh):
    in_specs = (
        P("ctx", "tp"),
        P(("ctx", "tp"), None),
        P("tp", None),
        P("tp", None),
        P(),
        P(),
        P(("ctx", "tp"), None),
        P(("ctx", "tp"), None),
        P(("ctx", "tp"), None, None),
        P(("ctx", "tp"), None, None),
        P(("ctx", "tp"), None, None),
        P("ctx", "tp"),
        P(("ctx", "tp"), None),
    )
    out_specs = (
        P("ctx", "tp"),
        P(("ctx", "tp"), None),
        P("ctx", "tp"),
        P(("ctx", "tp"), None),
        P("tp", "ctx"),
        P(("ctx", "tp"), None, None),
        P(("ctx", "tp"), None, None),
        P(("ctx", "tp"), None, None),
    )
    return jax.shard_map(local, mesh=mesh, in_specs=in_specs, out_specs=out_specs, check_vma=False)
```

```python
import functools

import jax
import jax.numpy as jnp
from jax import lax
from jax.experimental import pallas as pl
from jax.experimental.pallas import tpu as pltpu
from jax.sharding import PartitionSpec as P

MESH = pl.DeviceIdType.MESH
ROW_TILE = 16
COLUMN_TILE = 512
VMEM_BYTES = 40 * 1024 * 1024
LINK_COST = 32

EPSILON = 1e-06


def rms_inverse(hidden):
    return lax.rsqrt(jnp.mean(hidden * hidden, axis=-1, keepdims=True) + EPSILON)


def rms_grad(hidden, gain_vec, inv_rms, grad_out):
    normed = hidden * inv_rms
    grad_normed = grad_out * gain_vec
    return inv_rms * (grad_normed - normed * jnp.mean(grad_normed * normed, axis=-1, keepdims=True))


def expert_inner(slot_rows, gate_mat, up_mat):
    pre_gate = jnp.dot(slot_rows, gate_mat, preferred_element_type=jnp.float32)
    pre_up = jnp.dot(slot_rows, up_mat, preferred_element_type=jnp.float32)
    active = (jax.nn.silu(pre_gate) * pre_up).astype(jnp.bfloat16)
    return (pre_gate, pre_up, active)


def half_backward(slot_rows, slot_grads, pre_gate, pre_up, active, gate_mat, up_mat, down_mat):
    sigmoid_gate = jax.nn.sigmoid(pre_gate)
    silu_gate = pre_gate * sigmoid_gate
    grad_active = jnp.einsum("sd,fd->sf", slot_grads, down_mat, preferred_element_type=jnp.float32)
    grad_gate = (
        grad_active * pre_up * sigmoid_gate * (1.0 + pre_gate * (1.0 - sigmoid_gate))
    ).astype(jnp.bfloat16)
    grad_up = (grad_active * silu_gate).astype(jnp.bfloat16)
    input_part = jnp.einsum("sf,df->sd", grad_gate, gate_mat, preferred_element_type=jnp.float32)
    input_part = (
        input_part + jnp.einsum("sf,df->sd", grad_up, up_mat, preferred_element_type=jnp.float32)
    ).astype(jnp.bfloat16)
    gate_term = jnp.einsum("sd,sf->df", slot_rows, grad_gate, preferred_element_type=jnp.float32)
    up_term = jnp.einsum("sd,sf->df", slot_rows, grad_up, preferred_element_type=jnp.float32)
    down_term = jnp.einsum("sf,sd->fd", active, slot_grads, preferred_element_type=jnp.float32)
    return (input_part, gate_term, up_term, down_term)


def tensor_rows(local_sum):
    return lax.psum_scatter(
        local_sum.astype(jnp.bfloat16), "tp", scatter_dimension=0, tiled=True
    ).astype(jnp.float32)


def group_rows(local_rows):
    return lax.all_gather(local_rows, "tp", axis=0, tiled=True)


def greet(ctx_count, tensor_count, me_ctx, me_tp):
    barrier = pltpu.get_barrier_semaphore()
    for k in range(1, tensor_count):
        pl.semaphore_signal(
            barrier, inc=1, device_id=(me_ctx, (me_tp + k) % tensor_count), device_id_type=MESH
        )
    for m in range(1, ctx_count):
        pl.semaphore_signal(
            barrier, inc=1, device_id=((me_ctx + m) % ctx_count, me_tp), device_id_type=MESH
        )
    pl.semaphore_wait(barrier, tensor_count + ctx_count - 2)


def remote(src, dst, send_sem, recv_sem, device):
    return pltpu.make_async_remote_copy(
        src_ref=src,
        dst_ref=dst,
        send_sem=send_sem,
        recv_sem=recv_sem,
        device_id=device,
        device_id_type=MESH,
    )


def dispatch_kernel(
    ctx_count,
    tensor_count,
    cap,
    rows_ref,
    select_ref,
    scale_ref,
    out_ref,
    gathered,
    staged,
    z_send,
    z_recv,
    p_send,
    p_recv,
    own_sem,
):
    me_ctx, me_tp = lax.axis_index("ctx"), lax.axis_index("tp")
    width = rows_ref.shape[1]
    tile = min(COLUMN_TILE, width)
    greet(ctx_count, tensor_count, me_ctx, me_tp)
    along = [
        remote(
            rows_ref,
            gathered.at[k],
            z_send.at[k],
            z_recv.at[k],
            (me_ctx, (me_tp + k) % tensor_count),
        )
        for k in range(1, tensor_count)
    ]
    for copy in along:
        copy.start()
    plane, own = [], []
    for k in range(tensor_count):
        if k > 0:
            along[k - 1].wait_recv()
        for start in range(0, width, tile):
            columns = pl.ds(start, tile)
            rows = rows_ref[:, columns] if k == 0 else gathered[k, :, columns]
            picked = jnp.dot(select_ref[k], rows, preferred_element_type=jnp.float32)
            staged[k, :, columns] = (picked * scale_ref[k]).astype(jnp.bfloat16)
        for m in range(1, ctx_count):
            span = pl.ds(m * cap, cap)
            copy = remote(
                staged.at[k, span],
                out_ref.at[k, span],
                p_send.at[k, m],
                p_recv.at[k, m],
                ((me_ctx + m) % ctx_count, me_tp),
            )
            copy.start()
            plane.append(copy)
        span = pl.ds(0, cap)
        copy = pltpu.make_async_copy(staged.at[k, span], out_ref.at[k, span], own_sem.at[k])
        copy.start()
        own.append(copy)
    for copy in along:
        copy.wait_send()
    for copy in plane + own:
        copy.wait()


def combine_kernel(
    ctx_count,
    tensor_count,
    cap,
    slots_ref,
    weight_ref,
    out_ref,
    returned,
    partial,
    summed,
    z_send,
    z_recv,
    p_send,
    p_recv,
    own_sem,
):
    me_ctx, me_tp = lax.axis_index("ctx"), lax.axis_index("tp")
    width = out_ref.shape[1]
    tile = min(COLUMN_TILE, width)
    greet(ctx_count, tensor_count, me_ctx, me_tp)
    order = list(range(tensor_count - 1, -1, -1))
    plane, own = {}, {}
    for k in order:
        plane[k] = []
        for m in range(1, ctx_count):
            span = pl.ds(m * cap, cap)
            copy = remote(
                slots_ref.at[k, span],
                returned.at[k, span],
                p_send.at[k, m],
                p_recv.at[k, m],
                ((me_ctx + ctx_count - m) % ctx_count, me_tp),
            )
            copy.start()
            plane[k].append(copy)
        span = pl.ds(0, cap)
        own[k] = pltpu.make_async_copy(
            slots_ref.at[k, span], returned.at[k, span], own_sem.at[k]
        )
        own[k].start()
    along = []
    for k in order:
        for copy in plane[k]:
            copy.wait_recv()
        own[k].wait()
        for start in range(0, width, tile):
            columns = pl.ds(start, tile)
            total = jnp.dot(
                weight_ref[k], returned[k, :, columns], preferred_element_type=jnp.float32
            )
            if k == 0:
                out_ref[:, columns] = total
            else:
                partial[k, :, columns] = total.astype(jnp.bfloat16)
        if k > 0:
            copy = remote(
                partial.at[k],
                summed.at[k],
                z_send.at[k],
                z_recv.at[k],
                (me_ctx, (me_tp + tensor_count - k) % tensor_count),
            )
            copy.start()
            along.append(copy)
    for copy in along:
        copy.wait_recv()
    for start in range(0, width, tile):
        columns = pl.ds(start, tile)
        total = out_ref[:, columns]
        for k in range(1, tensor_count):
            total = total + summed[k, :, columns].astype(jnp.float32)
        out_ref[:, columns] = total
    for copy in along:
        copy.wait_send()
    for k in order:
        for copy in plane[k]:
            copy.wait_send()


def semaphores(ctx_count, tensor_count):
    return [
        pltpu.SemaphoreType.DMA((tensor_count,)),
        pltpu.SemaphoreType.DMA((tensor_count,)),
        pltpu.SemaphoreType.DMA((tensor_count, ctx_count)),
        pltpu.SemaphoreType.DMA((tensor_count, ctx_count)),
        pltpu.SemaphoreType.DMA((tensor_count,)),
    ]


def estimate(slots, tokens, width):
    return pl.CostEstimate(
        flops=2 * slots * tokens * width,
        bytes_accessed=2 * slots * width * LINK_COST,
        transcendentals=0,
    )


def dispatch(rows, select, scale, cap):
    ctx_count, tensor_count = lax.axis_size("ctx"), lax.axis_size("tp")
    tokens, width = rows.shape
    slots = select.shape[1]
    vmem = pl.BlockSpec(memory_space=pltpu.VMEM)
    return pl.pallas_call(
        functools.partial(dispatch_kernel, ctx_count, tensor_count, cap),
        out_shape=jax.ShapeDtypeStruct((tensor_count, slots, width), jnp.bfloat16),
        in_specs=[vmem] * 3,
        out_specs=pl.BlockSpec(memory_space=pl.ANY),
        scratch_shapes=[
            pltpu.VMEM((tensor_count, tokens, width), jnp.bfloat16),
            pltpu.VMEM((tensor_count, slots, width), jnp.bfloat16),
        ]
        + semaphores(ctx_count, tensor_count),
        compiler_params=pltpu.CompilerParams(
            collective_id=0, has_side_effects=True, vmem_limit_bytes=VMEM_BYTES
        ),
        cost_estimate=estimate(tensor_count * slots, tokens, width),
    )(rows, select, scale)


def combine(slot_rows, weights, cap):
    ctx_count, tensor_count = lax.axis_size("ctx"), lax.axis_size("tp")
    tokens, slots = weights.shape[1:]
    width = slot_rows.shape[2]
    vmem = pl.BlockSpec(memory_space=pltpu.VMEM)
    return pl.pallas_call(
        functools.partial(combine_kernel, ctx_count, tensor_count, cap),
        out_shape=jax.ShapeDtypeStruct((tokens, width), jnp.float32),
        in_specs=[pl.BlockSpec(memory_space=pl.ANY), vmem],
        out_specs=vmem,
        scratch_shapes=[
            pltpu.VMEM((tensor_count, slots, width), jnp.bfloat16),
            pltpu.VMEM((tensor_count, tokens, width), jnp.bfloat16),
            pltpu.VMEM((tensor_count, tokens, width), jnp.bfloat16),
        ]
        + semaphores(ctx_count, tensor_count),
        compiler_params=pltpu.CompilerParams(
            collective_id=1, has_side_effects=True, vmem_limit_bytes=VMEM_BYTES
        ),
        cost_estimate=estimate(tensor_count * slots, tokens, width),
    )(slot_rows, weights)


def local(
    attention,
    residual,
    w_out,
    w_qkv,
    norm_moe,
    norm_attn,
    expert_ids,
    expert_gates,
    w_gate,
    w_up,
    w_down,
    d_projected,
    d_stream,
):
    ctx_count = lax.axis_size("ctx")
    tensor_count = lax.axis_size("tp")
    local_tokens = residual.shape[0]
    model_width = residual.shape[1]
    expert_count = ctx_count * tensor_count // 2
    top_count = expert_ids.shape[1]
    capacity = 2 * max(1, local_tokens * top_count * 3 // (4 * expert_count))
    cap = -(-capacity // ROW_TILE) * ROW_TILE
    slots = ctx_count * cap
    me_ctx, me_tp = lax.axis_index("ctx"), lax.axis_index("tp")
    gate_mat = w_gate[0]
    up_mat = w_up[0]
    down_mat = w_down[0]

    routing = jnp.concatenate([expert_ids.astype(jnp.float32), expert_gates], axis=1)
    blocks = jnp.stack(
        [routing]
        + [
            lax.ppermute(
                routing, "tp", [(i, (i + k) % tensor_count) for i in range(tensor_count)]
            )
            for k in range(1, tensor_count)
        ]
    )
    ids = blocks[:, :, :top_count].astype(jnp.int32)
    gates = blocks[:, :, top_count:]
    peers = (me_ctx + jnp.arange(ctx_count, dtype=jnp.int32)) % ctx_count
    targets = (peers * tensor_count + me_tp) // 2
    named = ids[:, None, :, :] == targets[None, :, None, None]
    member = jnp.any(named, axis=3)
    gate_of = jnp.sum(jnp.where(named, gates[:, None, :, :], 0.0), axis=3)
    token_range = jnp.arange(local_tokens, dtype=jnp.int32)
    earlier = (token_range[:, None] < token_range[None, :]).astype(jnp.bfloat16)
    position = jnp.dot(
        member.astype(jnp.bfloat16), earlier, preferred_element_type=jnp.float32
    ).astype(jnp.int32)
    slot_of = jnp.where(member, position, -1)
    taken = slot_of[:, :, None, :] == jnp.arange(cap, dtype=jnp.int32)[None, None, :, None]
    select = taken.astype(jnp.bfloat16).reshape(tensor_count, slots, local_tokens)
    slot_gate = jnp.sum(jnp.where(taken, gate_of[:, :, None, :], 0.0), axis=3)
    slot_gate = slot_gate.reshape(tensor_count, slots, 1)
    select_back = jnp.swapaxes(select, 1, 2)
    gated_back = select_back * jnp.swapaxes(slot_gate, 1, 2).astype(jnp.bfloat16)

    def flat(rows):
        return rows.reshape(tensor_count * slots, model_width)

    def blocked(rows):
        return rows.reshape(tensor_count, slots, model_width)

    hidden = residual.astype(jnp.float32) + tensor_rows(
        jnp.dot(attention, w_out, preferred_element_type=jnp.float32)
    )
    inv_one = rms_inverse(hidden)
    moe_input = (hidden * inv_one * norm_moe).astype(jnp.bfloat16)
    moe_input, d_projected = lax.optimization_barrier((moe_input, d_projected))
    grad_attn_in = tensor_rows(
        jnp.dot(d_projected, w_qkv, preferred_element_type=jnp.float32)
    )
    arrived = flat(dispatch(moe_input, select, jnp.ones_like(slot_gate), cap))
    pre_gate, pre_up, active = expert_inner(arrived, gate_mat, up_mat)
    half_out = jnp.dot(active, down_mat, preferred_element_type=jnp.float32).astype(jnp.bfloat16)
    half_out, grad_attn_in = lax.optimization_barrier((half_out, grad_attn_in))
    stream_sum = hidden + combine(blocked(half_out), gated_back, cap)
    stream = stream_sum.astype(jnp.bfloat16)
    inv_two = rms_inverse(stream_sum)
    grad_stream = d_stream.astype(jnp.float32) + rms_grad(
        stream_sum, norm_attn, inv_two, grad_attn_in
    )
    attn_rows = group_rows((stream_sum * inv_two * norm_attn).astype(jnp.bfloat16))
    grad_arrived = flat(dispatch(grad_stream.astype(jnp.bfloat16), select, slot_gate, cap))
    input_part, gate_grad, up_grad, down_grad = half_backward(
        arrived, grad_arrived, pre_gate, pre_up, active, gate_mat, up_mat, down_mat
    )
    input_part, attn_rows = lax.optimization_barrier((input_part, attn_rows))
    projected = jnp.einsum(
        "td,od->to", attn_rows, w_qkv, preferred_element_type=jnp.float32
    ).astype(jnp.bfloat16)
    grad_moe_in = combine(blocked(input_part), select_back, cap)
    grad_hidden = grad_stream + rms_grad(hidden, norm_moe, inv_one, grad_moe_in)
    grad_residual = grad_hidden.astype(jnp.bfloat16)
    grad_rows_all = group_rows(grad_residual)
    grad_attention = jnp.einsum(
        "td,kd->tk", grad_rows_all, w_out, preferred_element_type=jnp.float32
    ).astype(jnp.bfloat16)
    out_partial = jnp.einsum(
        "tk,td->kd", attention, grad_rows_all, preferred_element_type=jnp.float32
    )
    out_weight_grad = lax.psum_scatter(
        out_partial, "ctx", scatter_dimension=1, tiled=True
    ).astype(jnp.bfloat16)
    return (
        projected,
        stream,
        grad_attention,
        grad_residual,
        out_weight_grad,
        gate_grad.astype(jnp.bfloat16)[None],
        up_grad.astype(jnp.bfloat16)[None],
        down_grad.astype(jnp.bfloat16)[None],
    )


def solution(mesh):
    in_specs = (
        P("ctx", "tp"),
        P(("ctx", "tp"), None),
        P("tp", None),
        P("tp", None),
        P(),
        P(),
        P(("ctx", "tp"), None),
        P(("ctx", "tp"), None),
        P(("ctx", "tp"), None, None),
        P(("ctx", "tp"), None, None),
        P(("ctx", "tp"), None, None),
        P("ctx", "tp"),
        P(("ctx", "tp"), None),
    )
    out_specs = (
        P("ctx", "tp"),
        P(("ctx", "tp"), None),
        P("ctx", "tp"),
        P(("ctx", "tp"), None),
        P("tp", "ctx"),
        P(("ctx", "tp"), None, None),
        P(("ctx", "tp"), None, None),
        P(("ctx", "tp"), None, None),
    )
    return jax.shard_map(local, mesh=mesh, in_specs=in_specs, out_specs=out_specs, check_vma=False)
```

```python
import functools

import jax
import jax.numpy as jnp
from jax import lax
from jax.experimental import pallas as pl
from jax.experimental.pallas import tpu as pltpu
from jax.sharding import PartitionSpec as P

MESH = pl.DeviceIdType.MESH
ROW_TILE = 16
COLUMN_TILE = 512
VMEM_BYTES = 40 * 1024 * 1024
LINK_COST = 32

EPSILON = 1e-06


def rms_inverse(hidden):
    return lax.rsqrt(jnp.mean(hidden * hidden, axis=-1, keepdims=True) + EPSILON)


def rms_grad(hidden, gain_vec, inv_rms, grad_out):
    normed = hidden * inv_rms
    grad_normed = grad_out * gain_vec
    return inv_rms * (grad_normed - normed * jnp.mean(grad_normed * normed, axis=-1, keepdims=True))


def expert_inner(slot_rows, gate_mat, up_mat):
    pre_gate = jnp.dot(slot_rows, gate_mat, preferred_element_type=jnp.float32)
    pre_up = jnp.dot(slot_rows, up_mat, preferred_element_type=jnp.float32)
    active = (jax.nn.silu(pre_gate) * pre_up).astype(jnp.bfloat16)
    return (pre_gate, pre_up, active)


def half_backward(slot_rows, slot_grads, pre_gate, pre_up, active, gate_mat, up_mat, down_mat):
    sigmoid_gate = jax.nn.sigmoid(pre_gate)
    silu_gate = pre_gate * sigmoid_gate
    grad_active = jnp.einsum("sd,fd->sf", slot_grads, down_mat, preferred_element_type=jnp.float32)
    grad_gate = (
        grad_active * pre_up * sigmoid_gate * (1.0 + pre_gate * (1.0 - sigmoid_gate))
    ).astype(jnp.bfloat16)
    grad_up = (grad_active * silu_gate).astype(jnp.bfloat16)
    input_part = jnp.einsum("sf,df->sd", grad_gate, gate_mat, preferred_element_type=jnp.float32)
    input_part = (
        input_part + jnp.einsum("sf,df->sd", grad_up, up_mat, preferred_element_type=jnp.float32)
    ).astype(jnp.bfloat16)
    gate_term = jnp.einsum("sd,sf->df", slot_rows, grad_gate, preferred_element_type=jnp.float32)
    up_term = jnp.einsum("sd,sf->df", slot_rows, grad_up, preferred_element_type=jnp.float32)
    down_term = jnp.einsum("sf,sd->fd", active, slot_grads, preferred_element_type=jnp.float32)
    return (input_part, gate_term, up_term, down_term)


def tensor_rows(local_sum):
    return lax.psum_scatter(
        local_sum.astype(jnp.bfloat16), "tp", scatter_dimension=0, tiled=True
    ).astype(jnp.float32)


def group_rows(local_rows):
    return lax.all_gather(local_rows, "tp", axis=0, tiled=True)


def greet(ctx_count, tensor_count, me_ctx, me_tp):
    barrier = pltpu.get_barrier_semaphore()
    for k in range(1, tensor_count):
        pl.semaphore_signal(
            barrier, inc=1, device_id=(me_ctx, (me_tp + k) % tensor_count), device_id_type=MESH
        )
    for m in range(1, ctx_count):
        pl.semaphore_signal(
            barrier, inc=1, device_id=((me_ctx + m) % ctx_count, me_tp), device_id_type=MESH
        )
    pl.semaphore_wait(barrier, tensor_count + ctx_count - 2)


def near_first(tensor_count):
    return sorted(range(1, tensor_count), key=lambda k: (min(k, tensor_count - k), k))


def remote(src, dst, send_sem, recv_sem, device):
    return pltpu.make_async_remote_copy(
        src_ref=src,
        dst_ref=dst,
        send_sem=send_sem,
        recv_sem=recv_sem,
        device_id=device,
        device_id_type=MESH,
    )


def dispatch_kernel(
    ctx_count,
    tensor_count,
    cap,
    rows_ref,
    select_ref,
    scale_ref,
    out_ref,
    gathered,
    staged,
    z_send,
    z_recv,
    p_send,
    p_recv,
    own_sem,
):
    me_ctx, me_tp = lax.axis_index("ctx"), lax.axis_index("tp")
    width = rows_ref.shape[1]
    tile = min(COLUMN_TILE, width)
    greet(ctx_count, tensor_count, me_ctx, me_tp)
    along = {
        k: remote(
            rows_ref,
            gathered.at[k],
            z_send.at[k],
            z_recv.at[k],
            (me_ctx, (me_tp + k) % tensor_count),
        )
        for k in range(1, tensor_count)
    }
    order = [0] + near_first(tensor_count)
    plane, own = [], []
    for turn, k in enumerate(order):
        if k > 0:
            along[k].wait()
        if turn + 1 < tensor_count:
            along[order[turn + 1]].start()
        for start in range(0, width, tile):
            columns = pl.ds(start, tile)
            rows = rows_ref[:, columns] if k == 0 else gathered[k, :, columns]
            picked = jnp.dot(select_ref[k], rows, preferred_element_type=jnp.float32)
            staged[k, :, columns] = (picked * scale_ref[k]).astype(jnp.bfloat16)
        for m in range(1, ctx_count):
            span = pl.ds(m * cap, cap)
            copy = remote(
                staged.at[k, span],
                out_ref.at[k, span],
                p_send.at[k, m],
                p_recv.at[k, m],
                ((me_ctx + m) % ctx_count, me_tp),
            )
            copy.start()
            plane.append(copy)
        span = pl.ds(0, cap)
        copy = pltpu.make_async_copy(staged.at[k, span], out_ref.at[k, span], own_sem.at[k])
        copy.start()
        own.append(copy)
    for copy in plane + own:
        copy.wait()


def combine_kernel(
    ctx_count,
    tensor_count,
    cap,
    slots_ref,
    weight_ref,
    out_ref,
    returned,
    partial,
    summed,
    z_send,
    z_recv,
    p_send,
    p_recv,
    own_sem,
):
    me_ctx, me_tp = lax.axis_index("ctx"), lax.axis_index("tp")
    width = out_ref.shape[1]
    tile = min(COLUMN_TILE, width)
    greet(ctx_count, tensor_count, me_ctx, me_tp)
    order = near_first(tensor_count)[::-1] + [0]
    plane, own = {}, {}

    def send_back(k):
        plane[k] = []
        for m in range(1, ctx_count):
            span = pl.ds(m * cap, cap)
            copy = remote(
                slots_ref.at[k, span],
                returned.at[k, span],
                p_send.at[k, m],
                p_recv.at[k, m],
                ((me_ctx + ctx_count - m) % ctx_count, me_tp),
            )
            copy.start()
            plane[k].append(copy)
        span = pl.ds(0, cap)
        own[k] = pltpu.make_async_copy(
            slots_ref.at[k, span], returned.at[k, span], own_sem.at[k]
        )
        own[k].start()

    send_back(order[0])
    along = []
    for turn, k in enumerate(order):
        for copy in plane[k]:
            copy.wait_send()
        if turn + 1 < tensor_count:
            send_back(order[turn + 1])
        for copy in plane[k]:
            copy.wait_recv()
        own[k].wait()
        for start in range(0, width, tile):
            columns = pl.ds(start, tile)
            total = jnp.dot(
                weight_ref[k], returned[k, :, columns], preferred_element_type=jnp.float32
            )
            if k == 0:
                out_ref[:, columns] = total
            else:
                partial[k, :, columns] = total.astype(jnp.bfloat16)
        if k > 0:
            copy = remote(
                partial.at[k],
                summed.at[k],
                z_send.at[k],
                z_recv.at[k],
                (me_ctx, (me_tp + tensor_count - k) % tensor_count),
            )
            copy.start()
            along.append(copy)
    for copy in along:
        copy.wait_recv()
    for start in range(0, width, tile):
        columns = pl.ds(start, tile)
        total = out_ref[:, columns]
        for k in range(1, tensor_count):
            total = total + summed[k, :, columns].astype(jnp.float32)
        out_ref[:, columns] = total
    for copy in along:
        copy.wait_send()


def semaphores(ctx_count, tensor_count):
    return [
        pltpu.SemaphoreType.DMA((tensor_count,)),
        pltpu.SemaphoreType.DMA((tensor_count,)),
        pltpu.SemaphoreType.DMA((tensor_count, ctx_count)),
        pltpu.SemaphoreType.DMA((tensor_count, ctx_count)),
        pltpu.SemaphoreType.DMA((tensor_count,)),
    ]


def estimate(slots, tokens, width):
    return pl.CostEstimate(
        flops=2 * slots * tokens * width,
        bytes_accessed=2 * slots * width * LINK_COST,
        transcendentals=0,
    )


def dispatch(rows, select, scale, cap):
    ctx_count, tensor_count = lax.axis_size("ctx"), lax.axis_size("tp")
    tokens, width = rows.shape
    slots = select.shape[1]
    vmem = pl.BlockSpec(memory_space=pltpu.VMEM)
    return pl.pallas_call(
        functools.partial(dispatch_kernel, ctx_count, tensor_count, cap),
        out_shape=jax.ShapeDtypeStruct((tensor_count, slots, width), jnp.bfloat16),
        in_specs=[vmem] * 3,
        out_specs=pl.BlockSpec(memory_space=pl.ANY),
        scratch_shapes=[
            pltpu.VMEM((tensor_count, tokens, width), jnp.bfloat16),
            pltpu.VMEM((tensor_count, slots, width), jnp.bfloat16),
        ]
        + semaphores(ctx_count, tensor_count),
        compiler_params=pltpu.CompilerParams(
            collective_id=0, has_side_effects=True, vmem_limit_bytes=VMEM_BYTES
        ),
        cost_estimate=estimate(tensor_count * slots, tokens, width),
    )(rows, select, scale)


def combine(slot_rows, weights, cap):
    ctx_count, tensor_count = lax.axis_size("ctx"), lax.axis_size("tp")
    tokens, slots = weights.shape[1:]
    width = slot_rows.shape[2]
    vmem = pl.BlockSpec(memory_space=pltpu.VMEM)
    return pl.pallas_call(
        functools.partial(combine_kernel, ctx_count, tensor_count, cap),
        out_shape=jax.ShapeDtypeStruct((tokens, width), jnp.float32),
        in_specs=[pl.BlockSpec(memory_space=pl.ANY), vmem],
        out_specs=vmem,
        scratch_shapes=[
            pltpu.VMEM((tensor_count, slots, width), jnp.bfloat16),
            pltpu.VMEM((tensor_count, tokens, width), jnp.bfloat16),
            pltpu.VMEM((tensor_count, tokens, width), jnp.bfloat16),
        ]
        + semaphores(ctx_count, tensor_count),
        compiler_params=pltpu.CompilerParams(
            collective_id=1, has_side_effects=True, vmem_limit_bytes=VMEM_BYTES
        ),
        cost_estimate=estimate(tensor_count * slots, tokens, width),
    )(slot_rows, weights)


def local(
    attention,
    residual,
    w_out,
    w_qkv,
    norm_moe,
    norm_attn,
    expert_ids,
    expert_gates,
    w_gate,
    w_up,
    w_down,
    d_projected,
    d_stream,
):
    ctx_count = lax.axis_size("ctx")
    tensor_count = lax.axis_size("tp")
    local_tokens = residual.shape[0]
    model_width = residual.shape[1]
    expert_count = ctx_count * tensor_count // 2
    top_count = expert_ids.shape[1]
    capacity = 2 * max(1, local_tokens * top_count * 3 // (4 * expert_count))
    cap = -(-capacity // ROW_TILE) * ROW_TILE
    slots = ctx_count * cap
    me_ctx, me_tp = lax.axis_index("ctx"), lax.axis_index("tp")
    gate_mat = w_gate[0]
    up_mat = w_up[0]
    down_mat = w_down[0]

    routing = jnp.concatenate([expert_ids.astype(jnp.float32), expert_gates], axis=1)
    blocks = jnp.stack(
        [routing]
        + [
            lax.ppermute(
                routing, "tp", [(i, (i + k) % tensor_count) for i in range(tensor_count)]
            )
            for k in range(1, tensor_count)
        ]
    )
    ids = blocks[:, :, :top_count].astype(jnp.int32)
    gates = blocks[:, :, top_count:]
    peers = (me_ctx + jnp.arange(ctx_count, dtype=jnp.int32)) % ctx_count
    targets = (peers * tensor_count + me_tp) // 2
    named = ids[:, None, :, :] == targets[None, :, None, None]
    member = jnp.any(named, axis=3)
    gate_of = jnp.sum(jnp.where(named, gates[:, None, :, :], 0.0), axis=3)
    token_range = jnp.arange(local_tokens, dtype=jnp.int32)
    earlier = (token_range[:, None] < token_range[None, :]).astype(jnp.bfloat16)
    position = jnp.dot(
        member.astype(jnp.bfloat16), earlier, preferred_element_type=jnp.float32
    ).astype(jnp.int32)
    slot_of = jnp.where(member, position, -1)
    taken = slot_of[:, :, None, :] == jnp.arange(cap, dtype=jnp.int32)[None, None, :, None]
    select = taken.astype(jnp.bfloat16).reshape(tensor_count, slots, local_tokens)
    slot_gate = jnp.sum(jnp.where(taken, gate_of[:, :, None, :], 0.0), axis=3)
    slot_gate = slot_gate.reshape(tensor_count, slots, 1)
    select_back = jnp.swapaxes(select, 1, 2)
    gated_back = select_back * jnp.swapaxes(slot_gate, 1, 2).astype(jnp.bfloat16)

    def flat(rows):
        return rows.reshape(tensor_count * slots, model_width)

    def blocked(rows):
        return rows.reshape(tensor_count, slots, model_width)

    attended = tensor_rows(jnp.dot(attention, w_out, preferred_element_type=jnp.float32))
    grad_partial = jnp.dot(d_projected, w_qkv, preferred_element_type=jnp.float32).astype(
        jnp.bfloat16
    )
    attended, select, slot_gate, select_back, gated_back, grad_partial = lax.optimization_barrier(
        (attended, select, slot_gate, select_back, gated_back, grad_partial)
    )
    hidden = residual.astype(jnp.float32) + attended
    inv_one = rms_inverse(hidden)
    moe_input = (hidden * inv_one * norm_moe).astype(jnp.bfloat16)
    moe_input, grad_partial = lax.optimization_barrier((moe_input, grad_partial))
    grad_attn_in = tensor_rows(grad_partial)
    arrived = flat(dispatch(moe_input, select, jnp.ones_like(slot_gate), cap))
    pre_gate, pre_up, active = expert_inner(arrived, gate_mat, up_mat)
    half_out = jnp.dot(active, down_mat, preferred_element_type=jnp.float32).astype(jnp.bfloat16)
    half_out, grad_attn_in = lax.optimization_barrier((half_out, grad_attn_in))
    stream_sum = hidden + combine(blocked(half_out), gated_back, cap)
    stream = stream_sum.astype(jnp.bfloat16)
    inv_two = rms_inverse(stream_sum)
    grad_stream = d_stream.astype(jnp.float32) + rms_grad(
        stream_sum, norm_attn, inv_two, grad_attn_in
    )
    attn_rows = group_rows((stream_sum * inv_two * norm_attn).astype(jnp.bfloat16))
    grad_arrived = flat(dispatch(grad_stream.astype(jnp.bfloat16), select, slot_gate, cap))
    input_part, gate_grad, up_grad, down_grad = half_backward(
        arrived, grad_arrived, pre_gate, pre_up, active, gate_mat, up_mat, down_mat
    )
    input_part, attn_rows = lax.optimization_barrier((input_part, attn_rows))
    projected = jnp.einsum(
        "td,od->to", attn_rows, w_qkv, preferred_element_type=jnp.float32
    ).astype(jnp.bfloat16)
    grad_moe_in = combine(blocked(input_part), select_back, cap)
    grad_hidden = grad_stream + rms_grad(hidden, norm_moe, inv_one, grad_moe_in)
    grad_residual = grad_hidden.astype(jnp.bfloat16)
    grad_rows_all = group_rows(grad_residual)
    grad_attention = jnp.einsum(
        "td,kd->tk", grad_rows_all, w_out, preferred_element_type=jnp.float32
    ).astype(jnp.bfloat16)
    out_partial = jnp.einsum(
        "tk,td->kd", attention, grad_rows_all, preferred_element_type=jnp.float32
    )
    out_weight_grad = lax.psum_scatter(
        out_partial, "ctx", scatter_dimension=1, tiled=True
    ).astype(jnp.bfloat16)
    return (
        projected,
        stream,
        grad_attention,
        grad_residual,
        out_weight_grad,
        gate_grad.astype(jnp.bfloat16)[None],
        up_grad.astype(jnp.bfloat16)[None],
        down_grad.astype(jnp.bfloat16)[None],
    )


def solution(mesh):
    in_specs = (
        P("ctx", "tp"),
        P(("ctx", "tp"), None),
        P("tp", None),
        P("tp", None),
        P(),
        P(),
        P(("ctx", "tp"), None),
        P(("ctx", "tp"), None),
        P(("ctx", "tp"), None, None),
        P(("ctx", "tp"), None, None),
        P(("ctx", "tp"), None, None),
        P("ctx", "tp"),
        P(("ctx", "tp"), None),
    )
    out_specs = (
        P("ctx", "tp"),
        P(("ctx", "tp"), None),
        P("ctx", "tp"),
        P(("ctx", "tp"), None),
        P("tp", "ctx"),
        P(("ctx", "tp"), None, None),
        P(("ctx", "tp"), None, None),
        P(("ctx", "tp"), None, None),
    )
    return jax.shard_map(local, mesh=mesh, in_specs=in_specs, out_specs=out_specs, check_vma=False)
```

```python
import functools

import jax
import jax.numpy as jnp
from jax import lax
from jax.experimental import pallas as pl
from jax.experimental.pallas import tpu as pltpu
from jax.sharding import PartitionSpec as P

MESH = pl.DeviceIdType.MESH
ROW_TILE = 16
COLUMN_TILE = 512
VMEM_BYTES = 40 * 1024 * 1024
LINK_COST = 32

EPSILON = 1e-06


def rms_inverse(hidden):
    return lax.rsqrt(jnp.mean(hidden * hidden, axis=-1, keepdims=True) + EPSILON)


def rms_grad(hidden, gain_vec, inv_rms, grad_out):
    normed = hidden * inv_rms
    grad_normed = grad_out * gain_vec
    return inv_rms * (grad_normed - normed * jnp.mean(grad_normed * normed, axis=-1, keepdims=True))


def expert_inner(slot_rows, gate_mat, up_mat):
    pre_gate = jnp.dot(slot_rows, gate_mat, preferred_element_type=jnp.float32)
    pre_up = jnp.dot(slot_rows, up_mat, preferred_element_type=jnp.float32)
    active = (jax.nn.silu(pre_gate) * pre_up).astype(jnp.bfloat16)
    return (pre_gate, pre_up, active)


def half_backward(slot_rows, slot_grads, pre_gate, pre_up, active, gate_mat, up_mat, down_mat):
    sigmoid_gate = jax.nn.sigmoid(pre_gate)
    silu_gate = pre_gate * sigmoid_gate
    grad_active = jnp.einsum("sd,fd->sf", slot_grads, down_mat, preferred_element_type=jnp.float32)
    grad_gate = (
        grad_active * pre_up * sigmoid_gate * (1.0 + pre_gate * (1.0 - sigmoid_gate))
    ).astype(jnp.bfloat16)
    grad_up = (grad_active * silu_gate).astype(jnp.bfloat16)
    input_part = jnp.einsum("sf,df->sd", grad_gate, gate_mat, preferred_element_type=jnp.float32)
    input_part = (
        input_part + jnp.einsum("sf,df->sd", grad_up, up_mat, preferred_element_type=jnp.float32)
    ).astype(jnp.bfloat16)
    gate_term = jnp.einsum("sd,sf->df", slot_rows, grad_gate, preferred_element_type=jnp.float32)
    up_term = jnp.einsum("sd,sf->df", slot_rows, grad_up, preferred_element_type=jnp.float32)
    down_term = jnp.einsum("sf,sd->fd", active, slot_grads, preferred_element_type=jnp.float32)
    return (input_part, gate_term, up_term, down_term)


def tensor_rows(local_sum):
    return lax.psum_scatter(
        local_sum.astype(jnp.bfloat16), "tp", scatter_dimension=0, tiled=True
    ).astype(jnp.float32)


def group_rows(local_rows):
    return lax.all_gather(local_rows, "tp", axis=0, tiled=True)


def greet(ctx_count, tensor_count, me_ctx, me_tp):
    barrier = pltpu.get_barrier_semaphore()
    for k in range(1, tensor_count):
        pl.semaphore_signal(
            barrier, inc=1, device_id=(me_ctx, (me_tp + k) % tensor_count), device_id_type=MESH
        )
    for m in range(1, ctx_count):
        pl.semaphore_signal(
            barrier, inc=1, device_id=((me_ctx + m) % ctx_count, me_tp), device_id_type=MESH
        )
    pl.semaphore_wait(barrier, tensor_count + ctx_count - 2)


def near_first(tensor_count):
    return sorted(range(1, tensor_count), key=lambda k: (min(k, tensor_count - k), k))


def remote(src, dst, send_sem, recv_sem, device):
    return pltpu.make_async_remote_copy(
        src_ref=src,
        dst_ref=dst,
        send_sem=send_sem,
        recv_sem=recv_sem,
        device_id=device,
        device_id_type=MESH,
    )


def dispatch_kernel(
    ctx_count,
    tensor_count,
    cap,
    rows_ref,
    select_ref,
    scale_ref,
    out_ref,
    gathered,
    staged,
    z_send,
    z_recv,
    p_send,
    p_recv,
    own_sem,
):
    me_ctx, me_tp = lax.axis_index("ctx"), lax.axis_index("tp")
    width = rows_ref.shape[1]
    tile = min(COLUMN_TILE, width)
    greet(ctx_count, tensor_count, me_ctx, me_tp)
    along = {
        k: remote(
            rows_ref,
            gathered.at[k],
            z_send.at[k],
            z_recv.at[k],
            (me_ctx, (me_tp + k) % tensor_count),
        )
        for k in range(1, tensor_count)
    }
    order = [0] + near_first(tensor_count)
    plane, own = [], []
    for turn, k in enumerate(order):
        if k > 0:
            along[k].wait()
        if turn + 1 < tensor_count:
            along[order[turn + 1]].start()
        for start in range(0, width, tile):
            columns = pl.ds(start, tile)
            rows = rows_ref[:, columns] if k == 0 else gathered[k, :, columns]
            picked = jnp.dot(select_ref[k], rows, preferred_element_type=jnp.float32)
            staged[k, :, columns] = (picked * scale_ref[k]).astype(jnp.bfloat16)
        for m in range(1, ctx_count):
            span = pl.ds(m * cap, cap)
            copy = remote(
                staged.at[k, span],
                out_ref.at[k, span],
                p_send.at[k, m],
                p_recv.at[k, m],
                ((me_ctx + m) % ctx_count, me_tp),
            )
            copy.start()
            plane.append(copy)
        span = pl.ds(0, cap)
        copy = pltpu.make_async_copy(staged.at[k, span], out_ref.at[k, span], own_sem.at[k])
        copy.start()
        own.append(copy)
    for copy in plane + own:
        copy.wait()


def combine_kernel(
    ctx_count,
    tensor_count,
    cap,
    slots_ref,
    weight_ref,
    out_ref,
    returned,
    partial,
    summed,
    z_send,
    z_recv,
    p_send,
    p_recv,
    own_sem,
):
    me_ctx, me_tp = lax.axis_index("ctx"), lax.axis_index("tp")
    width = out_ref.shape[1]
    tile = min(COLUMN_TILE, width)
    greet(ctx_count, tensor_count, me_ctx, me_tp)
    order = near_first(tensor_count)[::-1] + [0]
    plane, own = {}, {}

    def send_back(k):
        plane[k] = []
        for m in range(1, ctx_count):
            span = pl.ds(m * cap, cap)
            copy = remote(
                slots_ref.at[k, span],
                returned.at[k, span],
                p_send.at[k, m],
                p_recv.at[k, m],
                ((me_ctx + ctx_count - m) % ctx_count, me_tp),
            )
            copy.start()
            plane[k].append(copy)
        span = pl.ds(0, cap)
        own[k] = pltpu.make_async_copy(
            slots_ref.at[k, span], returned.at[k, span], own_sem.at[k]
        )
        own[k].start()

    send_back(order[0])
    along = []
    for turn, k in enumerate(order):
        for copy in plane[k]:
            copy.wait_send()
        if turn + 1 < tensor_count:
            send_back(order[turn + 1])
        for copy in plane[k]:
            copy.wait_recv()
        own[k].wait()
        for start in range(0, width, tile):
            columns = pl.ds(start, tile)
            total = jnp.dot(
                weight_ref[k], returned[k, :, columns], preferred_element_type=jnp.float32
            )
            if k == 0:
                out_ref[:, columns] = total
            else:
                partial[k, :, columns] = total.astype(jnp.bfloat16)
        if k > 0:
            copy = remote(
                partial.at[k],
                summed.at[k],
                z_send.at[k],
                z_recv.at[k],
                (me_ctx, (me_tp + tensor_count - k) % tensor_count),
            )
            copy.start()
            along.append(copy)
    for copy in along:
        copy.wait_recv()
    for start in range(0, width, tile):
        columns = pl.ds(start, tile)
        total = out_ref[:, columns]
        for k in range(1, tensor_count):
            total = total + summed[k, :, columns].astype(jnp.float32)
        out_ref[:, columns] = total
    for copy in along:
        copy.wait_send()


def semaphores(ctx_count, tensor_count):
    return [
        pltpu.SemaphoreType.DMA((tensor_count,)),
        pltpu.SemaphoreType.DMA((tensor_count,)),
        pltpu.SemaphoreType.DMA((tensor_count, ctx_count)),
        pltpu.SemaphoreType.DMA((tensor_count, ctx_count)),
        pltpu.SemaphoreType.DMA((tensor_count,)),
    ]


def estimate(slots, tokens, width):
    return pl.CostEstimate(
        flops=2 * slots * tokens * width,
        bytes_accessed=2 * slots * width * LINK_COST,
        transcendentals=0,
    )


def dispatch(rows, select, scale, cap):
    ctx_count, tensor_count = lax.axis_size("ctx"), lax.axis_size("tp")
    tokens, width = rows.shape
    slots = select.shape[1]
    vmem = pl.BlockSpec(memory_space=pltpu.VMEM)
    return pl.pallas_call(
        functools.partial(dispatch_kernel, ctx_count, tensor_count, cap),
        out_shape=jax.ShapeDtypeStruct((tensor_count, slots, width), jnp.bfloat16),
        in_specs=[vmem] * 3,
        out_specs=pl.BlockSpec(memory_space=pl.ANY),
        scratch_shapes=[
            pltpu.VMEM((tensor_count, tokens, width), jnp.bfloat16),
            pltpu.VMEM((tensor_count, slots, width), jnp.bfloat16),
        ]
        + semaphores(ctx_count, tensor_count),
        compiler_params=pltpu.CompilerParams(
            collective_id=0, has_side_effects=True, vmem_limit_bytes=VMEM_BYTES
        ),
        cost_estimate=estimate(tensor_count * slots, tokens, width),
    )(rows, select, scale)


def combine(slot_rows, weights, cap):
    ctx_count, tensor_count = lax.axis_size("ctx"), lax.axis_size("tp")
    tokens, slots = weights.shape[1:]
    width = slot_rows.shape[2]
    vmem = pl.BlockSpec(memory_space=pltpu.VMEM)
    return pl.pallas_call(
        functools.partial(combine_kernel, ctx_count, tensor_count, cap),
        out_shape=jax.ShapeDtypeStruct((tokens, width), jnp.float32),
        in_specs=[pl.BlockSpec(memory_space=pl.ANY), vmem],
        out_specs=vmem,
        scratch_shapes=[
            pltpu.VMEM((tensor_count, slots, width), jnp.bfloat16),
            pltpu.VMEM((tensor_count, tokens, width), jnp.bfloat16),
            pltpu.VMEM((tensor_count, tokens, width), jnp.bfloat16),
        ]
        + semaphores(ctx_count, tensor_count),
        compiler_params=pltpu.CompilerParams(
            collective_id=1, has_side_effects=True, vmem_limit_bytes=VMEM_BYTES
        ),
        cost_estimate=estimate(tensor_count * slots, tokens, width),
    )(slot_rows, weights)


def local(
    attention,
    residual,
    w_out,
    w_qkv,
    norm_moe,
    norm_attn,
    expert_ids,
    expert_gates,
    w_gate,
    w_up,
    w_down,
    d_projected,
    d_stream,
):
    ctx_count = lax.axis_size("ctx")
    tensor_count = lax.axis_size("tp")
    local_tokens = residual.shape[0]
    model_width = residual.shape[1]
    expert_count = ctx_count * tensor_count // 2
    top_count = expert_ids.shape[1]
    capacity = 2 * max(1, local_tokens * top_count * 3 // (4 * expert_count))
    cap = -(-capacity // ROW_TILE) * ROW_TILE
    slots = ctx_count * cap
    me_ctx, me_tp = lax.axis_index("ctx"), lax.axis_index("tp")
    gate_mat = w_gate[0]
    up_mat = w_up[0]
    down_mat = w_down[0]

    routing = jnp.concatenate([expert_ids.astype(jnp.float32), expert_gates], axis=1)
    blocks = jnp.stack(
        [routing]
        + [
            lax.ppermute(
                routing, "tp", [(i, (i + k) % tensor_count) for i in range(tensor_count)]
            )
            for k in range(1, tensor_count)
        ]
    )
    ids = blocks[:, :, :top_count].astype(jnp.int32)
    gates = blocks[:, :, top_count:]
    peers = (me_ctx + jnp.arange(ctx_count, dtype=jnp.int32)) % ctx_count
    targets = (peers * tensor_count + me_tp) // 2
    named = ids[:, None, :, :] == targets[None, :, None, None]
    member = jnp.any(named, axis=3)
    gate_of = jnp.sum(jnp.where(named, gates[:, None, :, :], 0.0), axis=3)
    token_range = jnp.arange(local_tokens, dtype=jnp.int32)
    earlier = (token_range[:, None] < token_range[None, :]).astype(jnp.bfloat16)
    position = jnp.dot(
        member.astype(jnp.bfloat16), earlier, preferred_element_type=jnp.float32
    ).astype(jnp.int32)
    slot_of = jnp.where(member, position, -1)
    taken = slot_of[:, :, None, :] == jnp.arange(cap, dtype=jnp.int32)[None, None, :, None]
    select = taken.astype(jnp.bfloat16).reshape(tensor_count, slots, local_tokens)
    slot_gate = jnp.sum(jnp.where(taken, gate_of[:, :, None, :], 0.0), axis=3)
    slot_gate = slot_gate.reshape(tensor_count, slots, 1)
    select_back = jnp.swapaxes(select, 1, 2)
    gated_back = select_back * jnp.swapaxes(slot_gate, 1, 2).astype(jnp.bfloat16)

    def flat(rows):
        return rows.reshape(tensor_count * slots, model_width)

    def blocked(rows):
        return rows.reshape(tensor_count, slots, model_width)

    attended = tensor_rows(jnp.dot(attention, w_out, preferred_element_type=jnp.float32))
    grad_partial = jnp.dot(d_projected, w_qkv, preferred_element_type=jnp.float32).astype(
        jnp.bfloat16
    )
    attended, select, slot_gate, select_back, gated_back, grad_partial = lax.optimization_barrier(
        (attended, select, slot_gate, select_back, gated_back, grad_partial)
    )
    hidden = residual.astype(jnp.float32) + attended
    inv_one = rms_inverse(hidden)
    moe_input = (hidden * inv_one * norm_moe).astype(jnp.bfloat16)
    arrived = flat(dispatch(moe_input, select, jnp.ones_like(slot_gate), cap))
    arrived, grad_partial = lax.optimization_barrier((arrived, grad_partial))
    grad_attn_in = tensor_rows(grad_partial)
    pre_gate, pre_up, active = expert_inner(arrived, gate_mat, up_mat)
    half_out = jnp.dot(active, down_mat, preferred_element_type=jnp.float32).astype(jnp.bfloat16)
    stream_sum = hidden + combine(blocked(half_out), gated_back, cap)
    stream = stream_sum.astype(jnp.bfloat16)
    inv_two = rms_inverse(stream_sum)
    grad_stream = d_stream.astype(jnp.float32) + rms_grad(
        stream_sum, norm_attn, inv_two, grad_attn_in
    )
    attn_input = (stream_sum * inv_two * norm_attn).astype(jnp.bfloat16)
    grad_arrived = flat(dispatch(grad_stream.astype(jnp.bfloat16), select, slot_gate, cap))
    grad_arrived, attn_input = lax.optimization_barrier((grad_arrived, attn_input))
    attn_rows = group_rows(attn_input)
    input_part, gate_grad, up_grad, down_grad = half_backward(
        arrived, grad_arrived, pre_gate, pre_up, active, gate_mat, up_mat, down_mat
    )
    grad_moe_in = combine(blocked(input_part), select_back, cap)
    grad_moe_in, attn_rows = lax.optimization_barrier((grad_moe_in, attn_rows))
    projected = jnp.einsum(
        "td,od->to", attn_rows, w_qkv, preferred_element_type=jnp.float32
    ).astype(jnp.bfloat16)
    grad_hidden = grad_stream + rms_grad(hidden, norm_moe, inv_one, grad_moe_in)
    grad_residual = grad_hidden.astype(jnp.bfloat16)
    grad_rows_all = group_rows(grad_residual)
    grad_attention = jnp.einsum(
        "td,kd->tk", grad_rows_all, w_out, preferred_element_type=jnp.float32
    ).astype(jnp.bfloat16)
    out_partial = jnp.einsum(
        "tk,td->kd", attention, grad_rows_all, preferred_element_type=jnp.float32
    )
    out_weight_grad = lax.psum_scatter(
        out_partial, "ctx", scatter_dimension=1, tiled=True
    ).astype(jnp.bfloat16)
    return (
        projected,
        stream,
        grad_attention,
        grad_residual,
        out_weight_grad,
        gate_grad.astype(jnp.bfloat16)[None],
        up_grad.astype(jnp.bfloat16)[None],
        down_grad.astype(jnp.bfloat16)[None],
    )


def solution(mesh):
    in_specs = (
        P("ctx", "tp"),
        P(("ctx", "tp"), None),
        P("tp", None),
        P("tp", None),
        P(),
        P(),
        P(("ctx", "tp"), None),
        P(("ctx", "tp"), None),
        P(("ctx", "tp"), None, None),
        P(("ctx", "tp"), None, None),
        P(("ctx", "tp"), None, None),
        P("ctx", "tp"),
        P(("ctx", "tp"), None),
    )
    out_specs = (
        P("ctx", "tp"),
        P(("ctx", "tp"), None),
        P("ctx", "tp"),
        P(("ctx", "tp"), None),
        P("tp", "ctx"),
        P(("ctx", "tp"), None, None),
        P(("ctx", "tp"), None, None),
        P(("ctx", "tp"), None, None),
    )
    return jax.shard_map(local, mesh=mesh, in_specs=in_specs, out_specs=out_specs, check_vma=False)
```
